256 devices in a mesh: grp: 4 (over y), feat: 64 (over z, x, core).
Axes of the slice: x: 4, y: 4, z: 8, core: 2. Of those that a mesh axis runs over, the one named last changes fastest.
Arguments:
- acts: bfloat16 [4, 512, 4096], P('grp', 'feat'), may hold values from -6 to 6
- targets: bfloat16 [4, 512, 4096], P('grp', 'feat'), may hold values from -6 to 6
- enc_weight: bfloat16 [4, 4096, 8192], P('grp', None, 'feat'), may hold values from -0.09375 to 0.09375
- enc_bias: float32 [4, 8192], P('grp', 'feat'), may hold values from -3 to 3
- dec_weight: bfloat16 [4, 4, 8192, 4096], P('grp', None, 'feat'), may hold values from -0.0625 to 0.0625
- block_mask: int32 [4, 4, 64], P('grp', None, 'feat'), may hold values 0 or 1
Outputs:
- grad_enc: bfloat16 [4, 4096, 8192], P('grp', None, 'feat')
- grad_dec: bfloat16 [4, 4, 8192, 4096], P('grp', None, 'feat')
- error: bfloat16 [4, 512, 4096], P('grp', 'feat')
The draws below stay inside these ranges and needn't reach their ends.
All inputs are finite; a program needn't handle non-finite values. No bound on the sum of `block_mask` on one device may be relied on, other than what follows from the above.
Results may differ from the reference program's by a relative error of at most 0.013.
Values may be sent and summed in bfloat16 or wider, within the bound.
No kernel may reach another device: no remote copies, remote signals or barrier semaphores. Data moves between devices by JAX's collectives and lax.ppermute only.
A program may use at most 128 MiB of HBM per device.

```python
import math
import jax
import jax.numpy as jnp

D = 4096
BLK = 128
TOKENS = 512
LAYERS = 4
F_LAYER = 8192


def touch_ends(values, key, least, top_value):
    shape = values.shape
    index_at = [jax.random.randint(jax.random.fold_in(key, axis), (), 0, shape[axis]) for axis in range(len(shape))]
    values = values.at[tuple(index_at)].set(least)
    longest = shape.index(max(shape))
    index_at[longest] = (index_at[longest] + 1) % shape[longest]
    return values.at[tuple(index_at)].set(top_value)


def steps_of(key, extent, cuts, least, high):
    gain, own = 1.0, jax.random.fold_in(key, 6)
    for axis_at, shards_of in cuts:
        steps = jnp.exp(jax.random.uniform(jax.random.fold_in(own, axis_at), (shards_of,), jnp.float32, least / len(cuts), high / len(cuts)))
        gain = gain * jnp.repeat(steps, extent[axis_at] // shards_of).reshape([-1 if axis == axis_at else 1 for axis in range(len(extent))])
    return gain


def normal_values(key, dims, scale, bound, split=(), dtype=jnp.bfloat16):
    array = jax.random.normal(key, dims, jnp.float32) * scale
    if len(split) > 0:
        array = steps_of(key, dims, split, -0.22, 0.18) * array
    return jnp.clip(array, min=-bound, max=bound).astype(dtype)


def setup_inputs(seed: int = 0) -> dict:
    key_list = jax.random.split(jax.random.key(seed), 7)
    acts = normal_values(key_list[0], (LAYERS, TOKENS, D), 1.0, 6.0, ((0, 4), (1, 64)))
    targets = normal_values(key_list[1], (LAYERS, TOKENS, D), 1.0, 6.0, ((0, 4), (1, 64)))
    enc_weight = normal_values(key_list[2], (LAYERS, D, F_LAYER), D ** -0.5, 0.09375, ((0, 4), (2, 64)))
    enc_bias = normal_values(key_list[3], (LAYERS, F_LAYER), 0.5, 3.0, ((0, 4), (1, 64)), jnp.float32)
    dec_weight = normal_values(key_list[4], (LAYERS, LAYERS, F_LAYER, D), F_LAYER ** -0.5, 0.0625, ((0, 4), (2, 64)))
    block_mask = touch_ends((jax.random.randint(key_list[5], (LAYERS, TOKENS // BLK, F_LAYER // BLK), 0, 2) < 1).astype(jnp.int32), jax.random.fold_in(key_list[5], 1), 0, 1)
    return dict(acts=acts, targets=targets, enc_weight=enc_weight, enc_bias=enc_bias, dec_weight=dec_weight, block_mask=block_mask)


def silu_slope(values):
    sigma = jax.nn.sigmoid(values)
    return sigma * (1.0 + values * (1.0 - sigma))

def spread_mask(blocks):
    tok_blocks, feat_blocks = blocks.shape
    wide = jnp.broadcast_to(blocks[:, None, :, None], (tok_blocks, BLK, feat_blocks, BLK))
    return wide.reshape(tok_blocks * BLK, feat_blocks * BLK).astype(jnp.float32)

def reference(acts, targets, enc_weight, enc_bias, dec_weight, block_mask):
    norm_scale = 1.0 / math.sqrt(TOKENS)
    pre_list, live_list, feat_list = ([], [], [])
    for layer in range(LAYERS):
        pre_act = jnp.dot(acts[layer], enc_weight[layer], preferred_element_type=jnp.float32) + enc_bias[layer]
        live = spread_mask(block_mask[layer])
        pre_list.append(pre_act)
        live_list.append(live)
        feat_list.append((jax.nn.silu(pre_act) * live).astype(jnp.bfloat16))
    error_list = []
    dec_rows = []
    for target in range(LAYERS):
        recon = jnp.zeros((TOKENS, D), jnp.float32)
        for source in range(target + 1):
            recon = recon + jnp.dot(feat_list[source], dec_weight[target, source], preferred_element_type=jnp.float32)
        residual_err = (recon - targets[target].astype(jnp.float32)).astype(jnp.bfloat16)
        error_list.append(residual_err)
        grads = []
        for source in range(LAYERS):
            if source <= target:
                summed = jnp.dot(feat_list[source].T, residual_err, preferred_element_type=jnp.float32)
                grads.append((summed * norm_scale).astype(jnp.bfloat16))
            else:
                grads.append(jnp.zeros((F_LAYER, D), jnp.bfloat16))
        dec_rows.append(jnp.stack(grads))
    enc_list = []
    for source in range(LAYERS):
        grad_feat = jnp.zeros((TOKENS, F_LAYER), jnp.float32)
        for target in range(source, LAYERS):
            grad_feat = grad_feat + jnp.dot(error_list[target], dec_weight[target, source].T, preferred_element_type=jnp.float32)
        grad_pre = (grad_feat * live_list[source] * silu_slope(pre_list[source])).astype(jnp.bfloat16)
        summed = jnp.dot(acts[source].T, grad_pre, preferred_element_type=jnp.float32)
        enc_list.append((summed * norm_scale).astype(jnp.bfloat16))
    return (jnp.stack(enc_list), jnp.stack(dec_rows), jnp.stack(error_list))
```

```python
import math

import jax
import jax.numpy as jnp
from jax import lax
from jax.sharding import PartitionSpec as P

BLK = 128
TOKENS = 512
NZ, NX = 8, 4
F32, BF16 = jnp.float32, jnp.bfloat16


def place(z, x, c):
    return ((z % NZ) * NX + x % NX) * 2 + c


def ring(axis, sign):
    pairs = []
    for z in range(NZ):
        for x in range(NX):
            for c in range(2):
                step = sign * (1 - 2 * c)
                there = place(z + step, x, c) if axis == "z" else place(z, x + step, c)
                pairs.append((place(z, x, c), there))
    return pairs


SIBLING = [(f, f ^ 1) for f in range(2 * NZ * NX)]


def send(value, pairs):
    return lax.ppermute(value, "feat", pairs)


def cat(parts):
    return jnp.concatenate(parts, axis=0)


def add(a, b):
    return (a.astype(F32) + b.astype(F32)).astype(BF16)


def gather_phase(mine, other, axis, n):
    half, rows = n // 2, mine.shape[0]
    ahead = ring(axis, 1)
    now = cat([mine, other])
    got = [now]
    for _ in range(half - 1):
        now = send(now, ahead)
        got.append(now)
    last = send(now[:rows], ahead)
    swap = send(cat(got[1:] + [last]), SIBLING)
    swapped = [swap[i * rows : (i + 1) * rows] for i in range(2 * half - 1)]
    mines = [g[:rows] for g in got] + [last] + swapped[1:-1:2]
    others = [g[rows:] for g in got] + [swapped[-1]] + swapped[0:-1:2]
    return mines, others


def turned(pieces):
    half = len(pieces) // 2
    first = lax.axis_index("feat") % 2 == 0
    same = [pieces[0]] + pieces[1:half] + [pieces[half]] + pieces[half + 1 :]
    other = [pieces[0]] + pieces[half + 1 :] + [pieces[half]] + pieces[1:half]
    return [a if a is b else jnp.where(first, a, b) for a, b in zip(same, other)]


def gather(shard, first, second):
    sizes = {"z": NZ, "x": NX}
    other = send(shard, SIBLING)
    mines, others = gather_phase(shard, other, first, sizes[first])
    mines, others = gather_phase(cat(turned(mines)), cat(turned(others)), second, sizes[second])
    return cat([p for pair in zip(mines, others) for p in pair])


def scatter_phase(mines, others, axis, n):
    half, rows = n // 2, mines[0].shape[0]
    back = ring(axis, -1)
    out = []
    for k in range(1, half):
        out += [others[half + k], mines[half + k]]
    out += [others[half], others[0]]
    swap = send(cat(out), SIBLING)
    swapped = [swap[i * rows : (i + 1) * rows] for i in range(2 * half)]
    moving = send(add(mines[half], swapped[-2]), back)
    for k in range(half - 1, 0, -1):
        a = mines[k].astype(F32) + swapped[2 * k - 2].astype(F32)
        b = others[k].astype(F32) + swapped[2 * k - 1].astype(F32)
        a = a + moving[:rows].astype(F32)
        if k < half - 1:
            b = b + moving[rows:].astype(F32)
        moving = send(cat([a.astype(BF16), b.astype(BF16)]), back)
    mine = mines[0].astype(F32) + swapped[-1].astype(F32) + moving[:rows].astype(F32)
    return mine.astype(BF16), moving[rows:]


def split(value, n):
    rows = value.shape[0] // n
    return [value[i * rows : (i + 1) * rows] for i in range(n)]


def scatter(partial, first, second):
    sizes = {"z": NZ, "x": NX}
    pieces = split(partial, 2 * sizes[first])
    mine, other = scatter_phase(pieces[0::2], pieces[1::2], first, sizes[first])
    mines, others = turned(split(mine, sizes[second])), turned(split(other, sizes[second]))
    mine, other = scatter_phase(mines, others, second, sizes[second])
    return mine.astype(F32) + send(other, SIBLING).astype(F32)


def positions(n):
    half = n // 2
    return jnp.array([0] + [-k for k in range(1, half)] + [half] + list(range(1, half)), jnp.int32)


def tokens_of(here, first):
    z, x, c = here // (2 * NX), here // 2 % NX, here % 2
    way = 1 - 2 * c
    kind = jnp.stack([c, 1 - c])[None, :, None, None]
    row = jnp.arange(8, dtype=jnp.int32)[None, None, None, :]
    if first == "x":
        zs = ((z + way * positions(NZ)) % NZ)[:, None, None, None]
        xs = ((x + positions(NX)) % NX)[None, None, :, None]
    else:
        xs = ((x + way * positions(NX)) % NX)[:, None, None, None]
        zs = ((z + positions(NZ)) % NZ)[None, None, :, None]
    return (((zs * NX + xs) * 2 + kind) * 8 + row).reshape(TOKENS)


def silu_slope(values):
    sigma = jax.nn.sigmoid(values)
    return sigma * (1.0 + values * (1.0 - sigma))


def dot(a, b, dims):
    return lax.dot_general(a, b, ((dims[0], dims[1]), ((), ())), preferred_element_type=F32)


def local(acts, targets, enc_weight, enc_bias, dec_weight, block_mask):
    groups = lax.axis_size("grp")
    group = lax.axis_index("grp")
    here = lax.axis_index("feat")
    norm_scale = 1.0 / math.sqrt(TOKENS)
    width = acts.shape[2]
    cut = width // 2
    feats = enc_weight.shape[2]
    enc = enc_weight[0]
    dec = dec_weight[0].reshape(groups * feats, width)

    tok_a, tok_b = tokens_of(here, "x"), tokens_of(here, "z")
    swap = (tok_a[:, None] == tok_b[None, :]).astype(BF16)

    def b_to_a(value):
        high = value.astype(BF16)
        low = (value - high.astype(F32)).astype(BF16)
        both = dot(swap, jnp.concatenate([high, low], axis=1), ((1,), (0,)))
        return both[:, : value.shape[1]] + both[:, value.shape[1] :]

    def a_to_b(value):
        return dot(swap, value, ((0,), (0,))).astype(BF16)

    acts_a = gather(acts[0, :, :cut], "x", "z")
    acts_b = gather(acts[0, :, cut:], "z", "x")
    pre = dot(acts_a, enc[:cut], ((1,), (0,))) + b_to_a(dot(acts_b, enc[cut:], ((1,), (0,)))) + enc_bias

    blocks = block_mask[0, :, 0].astype(F32)
    live = jnp.sum(jnp.where((tok_a[:, None] // BLK) == jnp.arange(blocks.shape[0])[None, :], blocks[None, :], 0.0), axis=1, keepdims=True)

    features = (jax.nn.silu(pre) * live).astype(BF16)
    behind = [features]
    for k in range(1, groups):
        behind.append(lax.ppermute(features, "grp", [(g, g + k) for g in range(groups - k)]))
    stacked = jnp.stack(behind + behind[1:])[::-1]
    sources = [lax.dynamic_index_in_dim(stacked, (2 * groups - 2 - (group - l) % groups), 0, keepdims=False) for l in range(groups)]
    feats_a = jnp.concatenate(sources, axis=1)
    feats_b = a_to_b(feats_a)

    recon_a = dot(feats_a, dec[:, :cut], ((1,), (0,))).astype(BF16)
    recon_b = dot(feats_b, dec[:, cut:], ((1,), (0,))).astype(BF16)
    own_a = scatter(recon_a, "z", "x")
    own_b = scatter(recon_b, "x", "z")
    err_a = (own_a - targets[0, :, :cut].astype(F32)).astype(BF16)
    err_b = (own_b - targets[0, :, cut:].astype(F32)).astype(BF16)
    all_a = gather(err_a, "x", "z")
    all_b = gather(err_b, "z", "x")

    grad_a = dot(all_a, dec[:, :cut], ((1,), (1,)))
    grad_b = dot(all_b, dec[:, cut:], ((1,), (1,)))
    grads = grad_a + b_to_a(grad_b)
    parts = jnp.stack([grads[:, l * feats : (l + 1) * feats] for l in range(groups)])
    mine = lax.dynamic_index_in_dim(parts, group, 0, keepdims=False)
    sent = parts.astype(BF16)
    for k in range(1, groups):
        part = lax.dynamic_index_in_dim(sent, (group - k) % groups, 0, keepdims=False)
        mine = mine + lax.ppermute(part, "grp", [(g, g - k) for g in range(k, groups)]).astype(F32)
    grad_pre = (mine * live * silu_slope(pre)).astype(BF16)
    pre_b = a_to_b(grad_pre)

    dec_a = (dot(feats_a, all_a, ((0,), (0,))) * norm_scale).astype(BF16)
    dec_b = (dot(feats_b, all_b, ((0,), (0,))) * norm_scale).astype(BF16)
    grad_dec = jnp.concatenate([dec_a, dec_b], axis=1).reshape(groups, feats, width)[None]
    enc_a = (dot(acts_a, grad_pre, ((0,), (0,))) * norm_scale).astype(BF16)
    enc_b = (dot(acts_b, pre_b, ((0,), (0,))) * norm_scale).astype(BF16)
    grad_enc = jnp.concatenate([enc_a, enc_b], axis=0)[None]
    error = jnp.concatenate([err_a, err_b], axis=1)[None]
    return grad_enc, grad_dec, error


def solution(mesh):
    return jax.shard_map(
        local,
        mesh=mesh,
        in_specs=(
            P("grp", "feat", None),
            P("grp", "feat", None),
            P("grp", None, "feat"),
            P("grp", "feat"),
            P("grp", None, "feat", None),
            P("grp", None, "feat"),
        ),
        out_specs=(P("grp", None, "feat"), P("grp", None, "feat", None), P("grp", "feat", None)),
        check_vma=False,
    )
```

```python
import math

import jax
import jax.numpy as jnp
from jax import lax
from jax.sharding import PartitionSpec as P

BLK = 128
TOKENS = 512
NZ, NX = 8, 4
F32, BF16 = jnp.float32, jnp.bfloat16


def place(z, x, c):
    return ((z % NZ) * NX + x % NX) * 2 + c


def ring(axis, by):
    pairs = []
    for z in range(NZ):
        for x in range(NX):
            for c in range(2):
                step = by * (1 - 2 * c)
                there = place(z + step, x, c) if axis == "z" else place(z, x + step, c)
                pairs.append((place(z, x, c), there))
    return pairs


CHIP = [(0, 0, 0), (0, 0, 1)]
SIBLING = [(f, f ^ 1) for f in range(2 * NZ * NX)]


def norm(unit):
    dz, dx, kind = unit
    return (dz % NZ, dx % NX, kind)


def seen_by_sibling(units):
    return [norm((-dz, -dx, 1 - kind)) for dz, dx, kind in units]


def hop(piece, axis, by):
    value, units = piece
    got = lax.ppermute(value, "feat", ring(axis, by))
    if axis == "z":
        return got, [norm((dz - by, dx, kind)) for dz, dx, kind in units]
    return got, [norm((dz, dx - by, kind)) for dz, dx, kind in units]


def swap(piece):
    value, units = piece
    return lax.ppermute(value, "feat", SIBLING), seen_by_sibling(units)


def cat(pieces):
    return jnp.concatenate([v for v, _ in pieces], axis=0), [u for _, us in pieces for u in us]


def rows(piece, start, count):
    value, units = piece
    return value[start * 8 : (start + count) * 8], units[start : start + count]


def tokens_of(here, units):
    z, x, c = here // (2 * NX), here // 2 % NX, here % 2
    way = 1 - 2 * c
    dz = jnp.array([u[0] for u in units], jnp.int32)
    dx = jnp.array([u[1] for u in units], jnp.int32)
    kind = jnp.array([u[2] for u in units], jnp.int32)
    zs = (z + way * dz + NZ) % NZ
    xs = (x + way * dx + NX) % NX
    device = (zs * NX + xs) * 2 + (c + kind) % 2
    return (device[:, None] * 8 + jnp.arange(8, dtype=jnp.int32)[None, :]).reshape(-1)


def after(piece, others):
    value, others = lax.optimization_barrier((piece[0], others))
    return (value, piece[1]), others


def gather(chip_rows, use):
    now = (chip_rows, CHIP)
    mine = rows(now, 0, 1)
    first = cat([mine, hop(now, "z", 1), hop(now, "z", 2), hop(now, "z", 3), hop(mine, "z", 4)])
    second = swap(first)
    (one, two), units = lax.optimization_barrier((first[0], second[0])), (first[1], second[1])
    first, second = (one, units[0]), (two, units[1])
    near = hop(first, "x", 1)
    near2 = hop(second, "x", 1)
    near, used = after(near, [use(p[0]) for p in (first, second)])
    far = hop(near, "x", 1)
    middle = [near, near2, swap(near), swap(near2)]
    far, more = after(far, [use(p[0]) for p in middle])
    last = [far, swap(far)]
    pieces = [first, second] + middle + last
    return pieces, jnp.concatenate(used + more + [use(p[0]) for p in last], axis=0)


def plus(*parts):
    return sum([p.astype(F32) for p in parts[1:]], parts[0].astype(F32)).astype(BF16)


def scatter_lists():
    def at(dz, kinds):
        return [norm((dz, 0, kind)) for kind in kinds]

    keep = at(-3, (0, 1)) + at(4, (0,)) + at(-1, (0, 1)) + at(-2, (0, 1)) + at(0, (0,))
    give = seen_by_sibling(keep)

    def column(units, dx):
        return [norm((dz, dx, kind)) for dz, _, kind in units]

    return column(keep, 2) + column(give, -1) + column(keep, -1) + column(keep, 0)


def scatter(far_give, near):
    far = lax.ppermute(far_give[:64], "feat", ring("x", -1))
    give = lax.ppermute(far_give[64:], "feat", ring("x", -1))
    keep = lax.ppermute(plus(near[:64], far), "feat", ring("x", -1))
    keep = plus(keep, near[64:], lax.ppermute(give, "feat", SIBLING))
    three = lax.ppermute(keep[:16], "feat", ring("z", -3))
    four = lax.ppermute(keep[16:24], "feat", ring("z", -4))
    one = lax.ppermute(keep[24:40], "feat", ring("z", -1))
    two = lax.ppermute(keep[40:56], "feat", ring("z", -2))
    both = one.astype(F32) + two.astype(F32) + three.astype(F32)
    mine = both[:8] + four.astype(F32) + keep[56:].astype(F32)
    part = jnp.concatenate([mine, both[8:]], axis=0).astype(BF16)
    got = lax.ppermute(part, "feat", SIBLING)
    return part.astype(F32) + jnp.concatenate([got[8:], got[:8]], axis=0).astype(F32)


def silu_slope(values):
    sigma = jax.nn.sigmoid(values)
    return sigma * (1.0 + values * (1.0 - sigma))


def dot(a, b, dims=((1,), (0,))):
    return lax.dot_general(a, b, (dims, ((), ())), preferred_element_type=F32)


def local(acts, targets, enc_weight, enc_bias, dec_weight, block_mask):
    groups = lax.axis_size("grp")
    group = lax.axis_index("grp")
    here = lax.axis_index("feat")
    norm_scale = 1.0 / math.sqrt(TOKENS)
    width = acts.shape[2]
    feats = enc_weight.shape[2]
    enc = enc_weight[0]

    own = jnp.concatenate([acts[0], targets[0]], axis=0)
    sib = lax.ppermute(own, "feat", SIBLING)
    pieces, pre = gather(jnp.concatenate([own[:8], sib[:8]], axis=0), lambda v: dot(v, enc))
    targ16 = jnp.concatenate([own[8:], sib[8:]], axis=0).astype(F32)
    order_f = [u for _, us in pieces for u in us]
    pre = pre + enc_bias

    here, dec, blocks, _ = lax.optimization_barrier((here, dec_weight[0], block_mask[0, :, 0], pieces[0][0]))
    dec = jnp.concatenate([lax.dynamic_index_in_dim(dec, (group - k) % groups, 0, keepdims=False) for k in range(groups)], axis=0)
    tok_f = tokens_of(here, order_f)
    live = (tok_f[:, None] // BLK) == jnp.arange(blocks.shape[0])[None, :]
    live = jnp.sum(jnp.where(live, blocks[None, :].astype(F32), 0.0), axis=1, keepdims=True)
    keep = scatter_lists()
    tok_r = tokens_of(here, seen_by_sibling(keep) + keep)
    to_r = (tok_r[:, None] == tok_f[None, :]).astype(BF16)

    features = (jax.nn.silu(pre) * live).astype(BF16)
    feats_r = dot(to_r, features).astype(BF16)
    behind = [feats_r]
    for k in range(1, groups):
        behind.append(lax.ppermute(feats_r, "grp", [(g, g + k) for g in range(groups - k)]))
    feats_r = jnp.concatenate(behind, axis=1)

    give = dot(feats_r[:256], dec).astype(BF16)
    own_rows = dot(feats_r[256:], dec).astype(BF16)
    far_give = plus(own_rows[:128], lax.ppermute(give[:128], "feat", SIBLING))
    near = plus(own_rows[128:], lax.ppermute(give[128:], "feat", SIBLING))
    err16 = (scatter(far_give, near) - targ16).astype(BF16)
    errs, grads = gather(err16, lambda v: dot(v, dec, ((1,), (1,))))
    errs = [v for v, _ in errs]
    mine = grads[:, :feats]
    sent = grads.astype(BF16)
    for k in range(1, groups):
        part = sent[:, k * feats : (k + 1) * feats]
        mine = mine + lax.ppermute(part, "grp", [(g, g - k) for g in range(k, groups)]).astype(F32)
    grad_pre = (mine * live * silu_slope(pre)).astype(BF16)

    placed = jnp.stack(behind)
    placed = jnp.concatenate([lax.dynamic_index_in_dim(placed, (group - l) % groups, 0, keepdims=False) for l in range(groups)], axis=1)
    placed = dot(to_r, placed, ((0,), (0,))).astype(BF16)
    errs, sent = lax.optimization_barrier((errs, sent))
    grad_dec = (dot(placed, jnp.concatenate(errs, axis=0), ((0,), (0,))) * norm_scale).astype(BF16)
    grad_dec = grad_dec.reshape(groups, feats, width)[None]
    grad_enc = (dot(jnp.concatenate([v for v, _ in pieces], axis=0), grad_pre, ((0,), (0,))) * norm_scale).astype(BF16)[None]
    return grad_enc, grad_dec, err16[:8][None]


def solution(mesh):
    return jax.shard_map(
        local,
        mesh=mesh,
        in_specs=(
            P("grp", "feat", None),
            P("grp", "feat", None),
            P("grp", None, "feat"),
            P("grp", "feat"),
            P("grp", None, "feat", None),
            P("grp", None, "feat"),
        ),
        out_specs=(P("grp", None, "feat"), P("grp", None, "feat", None), P("grp", "feat", None)),
        check_vma=False,
    )
```

```python
import math

import jax
import jax.numpy as jnp
from jax import lax
from jax.sharding import PartitionSpec as P

BLK = 128
TOKENS = 512
NZ, NX = 8, 4
F32, BF16 = jnp.float32, jnp.bfloat16


def place(z, x, c):
    return ((z % NZ) * NX + x % NX) * 2 + c


def ring(axis, by):
    pairs = []
    for z in range(NZ):
        for x in range(NX):
            for c in range(2):
                step = by * (1 - 2 * c)
                there = place(z + step, x, c) if axis == "z" else place(z, x + step, c)
                pairs.append((place(z, x, c), there))
    return pairs


CHIP = [(0, 0, 0), (0, 0, 1)]
SIBLING = [(f, f ^ 1) for f in range(2 * NZ * NX)]


def norm(unit):
    dz, dx, kind = unit
    return (dz % NZ, dx % NX, kind)


def seen_by_sibling(units):
    return [norm((-dz, -dx, 1 - kind)) for dz, dx, kind in units]


def hop(piece, axis, by):
    value, units = piece
    got = lax.ppermute(value, "feat", ring(axis, by))
    if axis == "z":
        return got, [norm((dz - by, dx, kind)) for dz, dx, kind in units]
    return got, [norm((dz, dx - by, kind)) for dz, dx, kind in units]


def swap(piece):
    value, units = piece
    return lax.ppermute(value, "feat", SIBLING), seen_by_sibling(units)


def cat(pieces):
    return jnp.concatenate([v for v, _ in pieces], axis=0), [u for _, us in pieces for u in us]


def rows(piece, start, count):
    value, units = piece
    return value[start * 8 : (start + count) * 8], units[start : start + count]


def tokens_of(here, units):
    z, x, c = here // (2 * NX), here // 2 % NX, here % 2
    way = 1 - 2 * c
    dz = jnp.array([u[0] for u in units], jnp.int32)
    dx = jnp.array([u[1] for u in units], jnp.int32)
    kind = jnp.array([u[2] for u in units], jnp.int32)
    zs = (z + way * dz + NZ) % NZ
    xs = (x + way * dx + NX) % NX
    device = (zs * NX + xs) * 2 + (c + kind) % 2
    return (device[:, None] * 8 + jnp.arange(8, dtype=jnp.int32)[None, :]).reshape(-1)


def after(piece, others):
    value, others = lax.optimization_barrier((piece[0], others))
    return (value, piece[1]), others


def gather(chip_rows, use):
    now = (chip_rows, CHIP)
    mine = rows(now, 0, 1)
    first = cat([mine, hop(now, "z", 1), hop(now, "z", 2), hop(now, "z", 3), hop(mine, "z", 4)])
    second = swap(first)
    (one, two), units = lax.optimization_barrier((first[0], second[0])), (first[1], second[1])
    first, second = (one, units[0]), (two, units[1])
    near = hop(first, "x", 1)
    near2 = hop(second, "x", 1)
    near, used = after(near, [use(p[0]) for p in (first, second)])
    far = hop(near, "x", 1)
    middle = [near, near2, swap(near), swap(near2)]
    far, more = after(far, [use(p[0]) for p in middle])
    last = [far, swap(far)]
    pieces = [first, second] + middle + last
    return pieces, jnp.concatenate(used + more + [use(p[0]) for p in last], axis=0)


def plus(*parts):
    return sum([p.astype(F32) for p in parts[1:]], parts[0].astype(F32)).astype(BF16)


def scatter_lists():
    def at(dz, kinds):
        return [norm((dz, 0, kind)) for kind in kinds]

    keep = at(-3, (0, 1)) + at(4, (0,)) + at(-1, (0, 1)) + at(-2, (0, 1)) + at(0, (0,))
    give = seen_by_sibling(keep)

    def column(units, dx):
        return [norm((dz, dx, kind)) for dz, _, kind in units]

    return column(keep, 2) + column(give, -1) + column(keep, -1) + column(keep, 0)


def scatter(far_give, near):
    far = lax.ppermute(far_give[:64], "feat", ring("x", -1))
    give = lax.ppermute(far_give[64:], "feat", ring("x", -1))
    keep = lax.ppermute(plus(near[:64], far), "feat", ring("x", -1))
    keep = plus(keep, near[64:], lax.ppermute(give, "feat", SIBLING))
    three = lax.ppermute(keep[:16], "feat", ring("z", -3))
    four = lax.ppermute(keep[16:24], "feat", ring("z", -4))
    one = lax.ppermute(keep[24:40], "feat", ring("z", -1))
    two = lax.ppermute(keep[40:56], "feat", ring("z", -2))
    both = one.astype(F32) + two.astype(F32) + three.astype(F32)
    mine = both[:8] + four.astype(F32) + keep[56:].astype(F32)
    part = jnp.concatenate([mine, both[8:]], axis=0).astype(BF16)
    got = lax.ppermute(part, "feat", SIBLING)
    return part.astype(F32) + jnp.concatenate([got[8:], got[:8]], axis=0).astype(F32)


def silu_slope(values):
    sigma = jax.nn.sigmoid(values)
    return sigma * (1.0 + values * (1.0 - sigma))


def dot(a, b, dims=((1,), (0,))):
    return lax.dot_general(a, b, (dims, ((), ())), preferred_element_type=F32)


def local(acts, targets, enc_weight, enc_bias, dec_weight, block_mask):
    groups = lax.axis_size("grp")
    group = lax.axis_index("grp")
    here = lax.axis_index("feat")
    norm_scale = 1.0 / math.sqrt(TOKENS)
    width = acts.shape[2]
    feats = enc_weight.shape[2]
    enc = enc_weight[0]

    pieces, pre = gather(jnp.concatenate([acts[0], lax.ppermute(acts[0], "feat", SIBLING)], axis=0), lambda v: dot(v, enc))
    order_f = [u for _, us in pieces for u in us]
    pre = pre + enc_bias

    here, dec, blocks, targ, _ = lax.optimization_barrier((here, dec_weight[0], block_mask[0, :, 0], targets[0], pieces[0][0]))
    targ16 = jnp.concatenate([targ, lax.ppermute(targ, "feat", SIBLING)], axis=0).astype(F32)
    dec = jnp.concatenate([lax.dynamic_index_in_dim(dec, (group - k) % groups, 0, keepdims=False) for k in range(groups)], axis=0)
    tok_f = tokens_of(here, order_f)
    live = (tok_f[:, None] // BLK) == jnp.arange(blocks.shape[0])[None, :]
    live = jnp.sum(jnp.where(live, blocks[None, :].astype(F32), 0.0), axis=1, keepdims=True)
    keep = scatter_lists()
    tok_r = tokens_of(here, seen_by_sibling(keep) + keep)
    to_r = (tok_r[:, None] == tok_f[None, :]).astype(BF16)

    features = (jax.nn.silu(pre) * live).astype(BF16)
    feats_r = dot(to_r, features).astype(BF16)
    behind = [feats_r]
    for k in range(1, groups):
        behind.append(lax.ppermute(feats_r, "grp", [(g, g + k) for g in range(groups - k)]))
    feats_r = jnp.concatenate(behind, axis=1)

    give = dot(feats_r[:256], dec).astype(BF16)
    own_rows = dot(feats_r[256:], dec).astype(BF16)
    far_give = plus(own_rows[:128], lax.ppermute(give[:128], "feat", SIBLING))
    near = plus(own_rows[128:], lax.ppermute(give[128:], "feat", SIBLING))
    err16 = (scatter(far_give, near) - targ16).astype(BF16)
    errs, grads = gather(err16, lambda v: dot(v, dec, ((1,), (1,))))
    errs = [v for v, _ in errs]
    mine = grads[:, :feats]
    sent = grads.astype(BF16)
    for k in range(1, groups):
        part = sent[:, k * feats : (k + 1) * feats]
        mine = mine + lax.ppermute(part, "grp", [(g, g - k) for g in range(k, groups)]).astype(F32)
    grad_pre = lax.optimization_barrier((mine * live * silu_slope(pre)).astype(BF16))

    placed = jnp.stack(behind)
    placed = jnp.concatenate([lax.dynamic_index_in_dim(placed, (group - l) % groups, 0, keepdims=False) for l in range(groups)], axis=1)
    placed = dot(to_r, placed, ((0,), (0,))).astype(BF16)
    errs, sent, placed = lax.optimization_barrier((errs, sent, placed))
    grad_dec = (dot(placed, jnp.concatenate(errs, axis=0), ((0,), (0,))) * norm_scale).astype(BF16)
    grad_dec = grad_dec.reshape(groups, feats, width)[None]
    grad_enc = (dot(jnp.concatenate([v for v, _ in pieces], axis=0), grad_pre, ((0,), (0,))) * norm_scale).astype(BF16)[None]
    return grad_enc, grad_dec, err16[:8][None]


def solution(mesh):
    return jax.shard_map(
        local,
        mesh=mesh,
        in_specs=(
            P("grp", "feat", None),
            P("grp", "feat", None),
            P("grp", None, "feat"),
            P("grp", "feat"),
            P("grp", None, "feat", None),
            P("grp", None, "feat"),
        ),
        out_specs=(P("grp", None, "feat"), P("grp", None, "feat", None), P("grp", "feat", None)),
        check_vma=False,
    )
```

```python
import math

import jax
import jax.numpy as jnp
from jax import lax
from jax.sharding import PartitionSpec as P

BLK = 128
TOKENS = 512
NZ, NX = 8, 4
F32, BF16 = jnp.float32, jnp.bfloat16


def place(z, x, c):
    return ((z % NZ) * NX + x % NX) * 2 + c


def ring(axis, by):
    pairs = []
    for z in range(NZ):
        for x in range(NX):
            for c in range(2):
                step = by * (1 - 2 * c)
                there = place(z + step, x, c) if axis == "z" else place(z, x + step, c)
                pairs.append((place(z, x, c), there))
    return pairs


CHIP = [(0, 0, 0), (0, 0, 1)]
SIBLING = [(f, f ^ 1) for f in range(2 * NZ * NX)]


def norm(unit):
    dz, dx, kind = unit
    return (dz % NZ, dx % NX, kind)


def seen_by_sibling(units):
    return [norm((-dz, -dx, 1 - kind)) for dz, dx, kind in units]


def hop(piece, axis, by):
    value, units = piece
    got = lax.ppermute(value, "feat", ring(axis, by))
    if axis == "z":
        return got, [norm((dz - by, dx, kind)) for dz, dx, kind in units]
    return got, [norm((dz, dx - by, kind)) for dz, dx, kind in units]


def swap(piece):
    value, units = piece
    return lax.ppermute(value, "feat", SIBLING), seen_by_sibling(units)


def cat(pieces):
    return jnp.concatenate([v for v, _ in pieces], axis=0), [u for _, us in pieces for u in us]


def rows(piece, start, count):
    value, units = piece
    return value[start * 8 : (start + count) * 8], units[start : start + count]


def tokens_of(here, units):
    z, x, c = here // (2 * NX), here // 2 % NX, here % 2
    way = 1 - 2 * c
    dz = jnp.array([u[0] for u in units], jnp.int32)
    dx = jnp.array([u[1] for u in units], jnp.int32)
    kind = jnp.array([u[2] for u in units], jnp.int32)
    zs = (z + way * dz + NZ) % NZ
    xs = (x + way * dx + NX) % NX
    device = (zs * NX + xs) * 2 + (c + kind) % 2
    return (device[:, None] * 8 + jnp.arange(8, dtype=jnp.int32)[None, :]).reshape(-1)


def after(piece, others):
    value, others = lax.optimization_barrier((piece[0], others))
    return (value, piece[1]), others


def gather(chip_rows, use):
    now = (chip_rows, CHIP)
    mine = rows(now, 0, 1)
    first = cat([mine, hop(now, "z", 1), hop(now, "z", 2), hop(now, "z", 3), hop(mine, "z", 4)])
    second = swap(first)
    (one, two), units = lax.optimization_barrier((first[0], second[0])), (first[1], second[1])
    first, second = (one, units[0]), (two, units[1])
    near = hop(first, "x", 1)
    near2 = hop(second, "x", 1)
    near, used = after(near, [use(p[0]) for p in (first, second)])
    far = hop(near, "x", 1)
    middle = [near, near2, swap(near), swap(near2)]
    far, more = after(far, [use(p[0]) for p in middle])
    last = [far, swap(far)]
    pieces = [first, second] + middle + last
    return pieces, jnp.concatenate(used + more + [use(p[0]) for p in last], axis=0)


def plus(*parts):
    return sum([p.astype(F32) for p in parts[1:]], parts[0].astype(F32)).astype(BF16)


def scatter_lists():
    def at(dz, kinds):
        return [norm((dz, 0, kind)) for kind in kinds]

    keep = at(-3, (0, 1)) + at(4, (0,)) + at(-1, (0, 1)) + at(-2, (0, 1)) + at(0, (0,))
    give = seen_by_sibling(keep)

    def column(units, dx):
        return [norm((dz, dx, kind)) for dz, _, kind in units]

    return column(keep, 2) + column(give, -1) + column(keep, -1) + column(keep, 0)


def scatter(far, give, near):
    far = lax.ppermute(far, "feat", ring("x", -1))
    give = lax.ppermute(give, "feat", ring("x", -1))
    passed = plus(near[:64], far)
    keep = lax.ppermute(passed, "feat", ring("x", -1))
    give, _ = lax.optimization_barrier((give, passed))
    keep = plus(keep, near[64:], lax.ppermute(give, "feat", SIBLING))
    three = lax.ppermute(keep[:16], "feat", ring("z", -3))
    four = lax.ppermute(keep[16:24], "feat", ring("z", -4))
    one = lax.ppermute(keep[24:40], "feat", ring("z", -1))
    two = lax.ppermute(keep[40:56], "feat", ring("z", -2))
    both = one.astype(F32) + two.astype(F32) + three.astype(F32)
    mine = both[:8] + four.astype(F32) + keep[56:].astype(F32)
    part = jnp.concatenate([mine, both[8:]], axis=0).astype(BF16)
    got = lax.ppermute(part, "feat", SIBLING)
    return part.astype(F32) + jnp.concatenate([got[8:], got[:8]], axis=0).astype(F32)


def silu_slope(values):
    sigma = jax.nn.sigmoid(values)
    return sigma * (1.0 + values * (1.0 - sigma))


def dot(a, b, dims=((1,), (0,))):
    return lax.dot_general(a, b, (dims, ((), ())), preferred_element_type=F32)


def local(acts, targets, enc_weight, enc_bias, dec_weight, block_mask):
    groups = lax.axis_size("grp")
    group = lax.axis_index("grp")
    here = lax.axis_index("feat")
    norm_scale = 1.0 / math.sqrt(TOKENS)
    width = acts.shape[2]
    feats = enc_weight.shape[2]
    enc = enc_weight[0]

    pieces, pre = gather(jnp.concatenate([acts[0], lax.ppermute(acts[0], "feat", SIBLING)], axis=0), lambda v: dot(v, enc))
    order_f = [u for _, us in pieces for u in us]
    pre = pre + enc_bias

    here, dec, blocks, targ, _ = lax.optimization_barrier((here, dec_weight[0], block_mask[0, :, 0], targets[0], pieces[0][0]))
    targ16 = jnp.concatenate([targ, lax.ppermute(targ, "feat", SIBLING)], axis=0).astype(F32)
    dec = jnp.concatenate([lax.dynamic_index_in_dim(dec, (group - k) % groups, 0, keepdims=False) for k in range(groups)], axis=0)
    tok_f = tokens_of(here, order_f)
    live = (tok_f[:, None] // BLK) == jnp.arange(blocks.shape[0])[None, :]
    live = jnp.sum(jnp.where(live, blocks[None, :].astype(F32), 0.0), axis=1, keepdims=True)
    keep = scatter_lists()
    tok_r = tokens_of(here, seen_by_sibling(keep) + keep)
    to_r = (tok_r[:, None] == tok_f[None, :]).astype(BF16)

    features = (jax.nn.silu(pre) * live).astype(BF16)
    feats_r = dot(to_r, features).astype(BF16)
    behind = [feats_r]
    for k in range(1, groups):
        behind.append(lax.ppermute(feats_r, "grp", [(g, g + k) for g in range(groups - k)]))
    feats_r = jnp.concatenate(behind, axis=1)

    halves = []
    for at in (0, 128):
        give = lax.ppermute(dot(feats_r[at : at + 128], dec).astype(BF16), "feat", SIBLING)
        halves.append((dot(feats_r[256 + at : 384 + at], dec).astype(BF16), give))
    far = plus(halves[0][0][:64], halves[0][1][:64])
    far, halves = lax.optimization_barrier((far, halves))
    give = plus(halves[0][0][64:], halves[0][1][64:])
    near = plus(*halves[1])
    give, near = lax.optimization_barrier((give, near))
    err16 = (scatter(far, give, near) - targ16).astype(BF16)
    errs, grads = gather(err16, lambda v: dot(v, dec, ((1,), (1,))))
    errs = [v for v, _ in errs]
    mine = grads[:, :feats]
    sent = grads.astype(BF16)
    for k in range(1, groups):
        part = sent[:, k * feats : (k + 1) * feats]
        mine = mine + lax.ppermute(part, "grp", [(g, g - k) for g in range(k, groups)]).astype(F32)
    grad_pre = lax.optimization_barrier((mine * live * silu_slope(pre)).astype(BF16))

    placed = jnp.stack(behind)
    placed = jnp.concatenate([lax.dynamic_index_in_dim(placed, (group - l) % groups, 0, keepdims=False) for l in range(groups)], axis=1)
    placed = dot(to_r, placed, ((0,), (0,))).astype(BF16)
    errs, sent, placed = lax.optimization_barrier((errs, sent, placed))
    grad_dec = (dot(placed, jnp.concatenate(errs, axis=0), ((0,), (0,))) * norm_scale).astype(BF16)
    grad_dec = grad_dec.reshape(groups, feats, width)[None]
    grad_enc = (dot(jnp.concatenate([v for v, _ in pieces], axis=0), grad_pre, ((0,), (0,))) * norm_scale).astype(BF16)[None]
    return grad_enc, grad_dec, err16[:8][None]


def solution(mesh):
    return jax.shard_map(
        local,
        mesh=mesh,
        in_specs=(
            P("grp", "feat", None),
            P("grp", "feat", None),
            P("grp", None, "feat"),
            P("grp", "feat"),
            P("grp", None, "feat", None),
            P("grp", None, "feat"),
        ),
        out_specs=(P("grp", None, "feat"), P("grp", None, "feat", None), P("grp", "feat", None)),
        check_vma=False,
    )
```

```python
import math

import jax
import jax.numpy as jnp
from jax import lax
from jax.sharding import PartitionSpec as P

BLK = 128
TOKENS = 512
NZ, NX = 8, 4
F32, BF16 = jnp.float32, jnp.bfloat16


def place(z, x, c):
    return ((z % NZ) * NX + x % NX) * 2 + c


def ring(axis, by):
    pairs = []
    for z in range(NZ):
        for x in range(NX):
            for c in range(2):
                step = by * (1 - 2 * c)
                there = place(z + step, x, c) if axis == "z" else place(z, x + step, c)
                pairs.append((place(z, x, c), there))
    return pairs


CHIP = [(0, 0, 0), (0, 0, 1)]
SIBLING = [(f, f ^ 1) for f in range(2 * NZ * NX)]


def norm(unit):
    dz, dx, kind = unit
    return (dz % NZ, dx % NX, kind)


def seen_by_sibling(units):
    return [norm((-dz, -dx, 1 - kind)) for dz, dx, kind in units]


def hop(piece, axis, by):
    value, units = piece
    got = lax.ppermute(value, "feat", ring(axis, by))
    if axis == "z":
        return got, [norm((dz - by, dx, kind)) for dz, dx, kind in units]
    return got, [norm((dz, dx - by, kind)) for dz, dx, kind in units]


def swap(piece):
    value, units = piece
    return lax.ppermute(value, "feat", SIBLING), seen_by_sibling(units)


def cat(pieces):
    return jnp.concatenate([v for v, _ in pieces], axis=0), [u for _, us in pieces for u in us]


def rows(piece, start, count):
    value, units = piece
    return value[start * 8 : (start + count) * 8], units[start : start + count]


def tokens_of(here, units):
    z, x, c = here // (2 * NX), here // 2 % NX, here % 2
    way = 1 - 2 * c
    dz = jnp.array([u[0] for u in units], jnp.int32)
    dx = jnp.array([u[1] for u in units], jnp.int32)
    kind = jnp.array([u[2] for u in units], jnp.int32)
    zs = (z + way * dz + NZ) % NZ
    xs = (x + way * dx + NX) % NX
    device = (zs * NX + xs) * 2 + (c + kind) % 2
    return (device[:, None] * 8 + jnp.arange(8, dtype=jnp.int32)[None, :]).reshape(-1)


def after(piece, others):
    value, others = lax.optimization_barrier((piece[0], others))
    return (value, piece[1]), others


def gather(mine, other, use):
    now = (jnp.concatenate([mine, other], axis=0), CHIP)
    mine = (mine, CHIP[:1])
    first = cat([mine, hop(now, "z", 1), hop(now, "z", 2), hop(now, "z", 3), hop(mine, "z", 4)])
    second = swap(first)
    (one, two), units = lax.optimization_barrier((first[0], second[0])), (first[1], second[1])
    first, second = (one, units[0]), (two, units[1])
    near = hop(first, "x", 1)
    near2 = hop(second, "x", 1)
    near, used = after(near, [use(p[0]) for p in (first, second)])
    far = hop(near, "x", 1)
    middle = [near, near2, swap(near), swap(near2)]
    far, more = after(far, [use(p[0]) for p in middle])
    last = [far, swap(far)]
    pieces = [first, second] + middle + last
    return pieces, jnp.concatenate(used + more + [use(p[0]) for p in last], axis=0)


def plus(*parts):
    return sum([p.astype(F32) for p in parts[1:]], parts[0].astype(F32)).astype(BF16)


def scatter_lists():
    def at(dz, kinds):
        return [norm((dz, 0, kind)) for kind in kinds]

    keep = at(-3, (0, 1)) + at(4, (0,)) + at(-1, (0, 1)) + at(-2, (0, 1)) + at(0, (0,))
    give = seen_by_sibling(keep)

    def column(units, dx):
        return [norm((dz, dx, kind)) for dz, _, kind in units]

    return column(keep, 2) + column(give, -1) + column(keep, -1) + column(keep, 0)


def scatter(far, give, near):
    far = lax.ppermute(far, "feat", ring("x", -1))
    give = lax.ppermute(give, "feat", ring("x", -1))
    passed = plus(near[:64], far)
    keep = lax.ppermute(passed, "feat", ring("x", -1))
    give, _ = lax.optimization_barrier((give, passed))
    keep = plus(keep, near[64:], lax.ppermute(give, "feat", SIBLING))
    three = lax.ppermute(keep[:16], "feat", ring("z", -3))
    four = lax.ppermute(keep[16:24], "feat", ring("z", -4))
    one = lax.ppermute(keep[24:40], "feat", ring("z", -1))
    two = lax.ppermute(keep[40:56], "feat", ring("z", -2))
    both = one.astype(F32) + two.astype(F32) + three.astype(F32)
    mine = both[:8] + four.astype(F32) + keep[56:].astype(F32)
    part = jnp.concatenate([mine, both[8:]], axis=0).astype(BF16)
    got = lax.ppermute(part, "feat", SIBLING)
    return part[:8].astype(F32) + got[8:].astype(F32), part[8:].astype(F32) + got[:8].astype(F32)


def silu_slope(values):
    sigma = jax.nn.sigmoid(values)
    return sigma * (1.0 + values * (1.0 - sigma))


def dot(a, b, dims=((1,), (0,))):
    return lax.dot_general(a, b, (dims, ((), ())), preferred_element_type=F32)


def local(acts, targets, enc_weight, enc_bias, dec_weight, block_mask):
    groups = lax.axis_size("grp")
    group = lax.axis_index("grp")
    here = lax.axis_index("feat")
    norm_scale = 1.0 / math.sqrt(TOKENS)
    width = acts.shape[2]
    feats = enc_weight.shape[2]
    enc = enc_weight[0]

    pieces, pre = gather(acts[0], lax.ppermute(acts[0], "feat", SIBLING), lambda v: dot(v, enc))
    order_f = [u for _, us in pieces for u in us]
    pre = pre + enc_bias

    here, dec, blocks, targ, _ = lax.optimization_barrier((here, dec_weight[0], block_mask[0, :, 0], targets[0], pieces[0][0]))
    targ_sib = lax.ppermute(targ, "feat", SIBLING)
    dec = jnp.concatenate([lax.dynamic_index_in_dim(dec, (group - k) % groups, 0, keepdims=False) for k in range(groups)], axis=0)
    tok_f = tokens_of(here, order_f)
    live = (tok_f[:, None] // BLK) == jnp.arange(blocks.shape[0])[None, :]
    live = jnp.sum(jnp.where(live, blocks[None, :].astype(F32), 0.0), axis=1, keepdims=True)
    keep = scatter_lists()
    tok_r = tokens_of(here, seen_by_sibling(keep) + keep)
    to_r = (tok_r[:, None] == tok_f[None, :]).astype(BF16)

    features = (jax.nn.silu(pre) * live).astype(BF16)
    feats_r = dot(to_r, features).astype(BF16)
    behind = [feats_r]
    for k in range(1, groups):
        behind.append(lax.ppermute(feats_r, "grp", [(g, g + k) for g in range(groups - k)]))
    feats_r = jnp.concatenate(behind, axis=1)

    halves = []
    for at in (0, 128):
        give = lax.ppermute(dot(feats_r[at : at + 128], dec).astype(BF16), "feat", SIBLING)
        halves.append((dot(feats_r[256 + at : 384 + at], dec).astype(BF16), give))
    far = plus(halves[0][0][:64], halves[0][1][:64])
    far, halves = lax.optimization_barrier((far, halves))
    give = plus(halves[0][0][64:], halves[0][1][64:])
    near = plus(*halves[1])
    give, near = lax.optimization_barrier((give, near))
    recon, recon_sib = scatter(far, give, near)
    err = (recon - targ.astype(F32)).astype(BF16)
    err_sib = (recon_sib - targ_sib.astype(F32)).astype(BF16)
    errs, grads = gather(err, err_sib, lambda v: dot(v, dec, ((1,), (1,))))
    errs = [v for v, _ in errs]
    mine = grads[:, :feats]
    sent = grads.astype(BF16)
    for k in range(1, groups):
        part = sent[:, k * feats : (k + 1) * feats]
        mine = mine + lax.ppermute(part, "grp", [(g, g - k) for g in range(k, groups)]).astype(F32)
    grad_pre = lax.optimization_barrier((mine * live * silu_slope(pre)).astype(BF16))

    placed = jnp.stack(behind)
    placed = jnp.concatenate([lax.dynamic_index_in_dim(placed, (group - l) % groups, 0, keepdims=False) for l in range(groups)], axis=1)
    placed = dot(to_r, placed, ((0,), (0,))).astype(BF16)
    errs, sent, placed = lax.optimization_barrier((errs, sent, placed))
    grad_dec = (dot(placed, jnp.concatenate(errs, axis=0), ((0,), (0,))) * norm_scale).astype(BF16)
    grad_dec = grad_dec.reshape(groups, feats, width)[None]
    grad_enc = (dot(jnp.concatenate([v for v, _ in pieces], axis=0), grad_pre, ((0,), (0,))) * norm_scale).astype(BF16)[None]
    return grad_enc, grad_dec, err[None]


def solution(mesh):
    return jax.shard_map(
        local,
        mesh=mesh,
        in_specs=(
            P("grp", "feat", None),
            P("grp", "feat", None),
            P("grp", None, "feat"),
            P("grp", "feat"),
            P("grp", None, "feat", None),
            P("grp", None, "feat"),
        ),
        out_specs=(P("grp", None, "feat"), P("grp", None, "feat", None), P("grp", "feat", None)),
        check_vma=False,
    )
```
